256 devices in a mesh: gx: 32 (over z, y), gy: 8 (over x, core).
Axes of the slice: x: 4, y: 4, z: 8, core: 2. Of those that a mesh axis runs over, the one named last changes fastest.
Arguments:
- section_start: float32 [5, 64, 256, 1024], P(None, None, 'gx', 'gy'), may hold values from -2 to 8, as said below
- section_now: float32 [5, 64, 256, 1024], P(None, None, 'gx', 'gy'), may hold values from -2 to 8, as said below
- history: bfloat16 [255, 16, 256, 1024], P(None, None, 'gx', 'gy'), may hold values from -9 to 9
Outputs:
- section_next: float32 [5, 64, 256, 1024], P(None, None, 'gx', 'gy')
- triangle: float32 [256, 256], replicated
The draws below stay inside these ranges and needn't reach their ends.
Inputs may be any that keep to these rules, and one draw needn't show every extreme that they name: `section_start`: component 0 lies in [1, 2], components 1 to 3 are density times a velocity of magnitude at most 1 in each direction, and component 4 is at least the kinetic energy. `section_now`: as section_start.
All inputs are finite; a program needn't handle non-finite values.
Results may differ from the reference program's by a relative error of at most 0.0003.
Values sent between devices are 32-bit elements; how exact they have to be, the bound alone decides.
A program may use at most 128 MiB of HBM per device.

```python
import math
import jax
import jax.numpy as jnp
from jax import lax

NZ = 64
CX = 8
SNAPS = 256
ZSUB = 4
NX = 256
NY = 1024
N_GX = 32


def draw_state(key):
    key_list = jax.random.split(key, 3)
    grid_shape = (NZ, NX, NY)
    density = jax.random.uniform(key_list[0], grid_shape, jnp.float32, 1.0, 2.0)
    velocity = jnp.clip(0.5 * jax.random.normal(key_list[1], (3,) + grid_shape, jnp.float32), -1.0, 1.0)
    pressure = jax.random.uniform(key_list[2], grid_shape, jnp.float32, 0.5, 2.0)
    momentum = density[None] * velocity
    energy = pressure / 0.4 + 0.5 * density * (velocity[0] * velocity[0] + velocity[1] * velocity[1] + velocity[2] * velocity[2])
    return jnp.concatenate([density[None], momentum, energy[None]], axis=0)


def draw_section_start(key, part):
    return draw_state(jax.random.fold_in(key, 11))


def draw_section_now(key, part):
    return draw_state(jax.random.fold_in(key, 23))


def draw_history(key, part):
    key_list = jax.random.split(jax.random.fold_in(key, 37), 3)
    grid_shape = (NZ // ZSUB, NX, NY)
    scales = 0.2 * jnp.exp(jax.random.uniform(key_list[0], grid_shape, jnp.float32, 0.0, math.log(10.0)))
    common = jnp.clip(jax.random.normal(key_list[1], grid_shape, jnp.float32), -3.0, 3.0)
    noise = jnp.clip(jax.random.normal(key_list[2], (SNAPS - 1,) + grid_shape, jnp.float32), -3.0, 3.0)
    values = scales[None] * (0.5 * common[None] + noise)
    return values.astype(jnp.bfloat16)


def setup_inputs(seed: int = 0) -> dict:
    streams_of = jax.random.split(jax.random.key(seed), 4)
    section_start = draw_section_start(jax.random.fold_in(streams_of[3], 71), 0)
    section_now = draw_section_now(jax.random.fold_in(streams_of[3], 71), 0)
    history = draw_history(jax.random.fold_in(streams_of[3], 71), 0)
    return {"section_start": section_start, "section_now": section_now, "history": history}


GAMMA_LESS = 0.4
TIME_STEP = 0.2
VISCOUS = 0.25
BLOCK_PLANES = 8

def pressure_of(fields):
    kinetic = fields[1] * fields[1] + fields[2] * fields[2] + fields[3] * fields[3]
    return GAMMA_LESS * (fields[4] - 0.5 * kinetic / fields[0])

def flux_of(fields, direction):
    velocity = fields[direction] / fields[0]
    pressure = pressure_of(fields)
    columns = [fields[member] * velocity for member in range(4)]
    columns[direction] = columns[direction] + pressure
    columns.append((fields[4] + pressure) * velocity)
    return jnp.stack(columns, axis=0)

def tendency_block(padded):
    center = padded[:, 1:-1]
    flux_x = flux_of(center, 1)
    flux_y = flux_of(center, 2)
    flux_z = flux_of(padded, 3)
    divergence = 0.5 * (jnp.roll(flux_x, -1, 2) - jnp.roll(flux_x, 1, 2))
    divergence = divergence + 0.5 * (jnp.roll(flux_y, -1, 3) - jnp.roll(flux_y, 1, 3))
    divergence = divergence + 0.5 * (flux_z[:, 2:] - flux_z[:, :-2])
    laplacian = jnp.roll(center, -1, 2) + jnp.roll(center, 1, 2)
    laplacian = laplacian + jnp.roll(center, -1, 3) + jnp.roll(center, 1, 3)
    laplacian = laplacian + padded[:, 2:] + padded[:, :-2] - 6.0 * center
    return VISCOUS * laplacian - divergence

def reference(section_start, section_now, history):
    padded = jnp.concatenate([section_now[:, :1], section_now, section_now[:, -1:]], axis=1)
    block_count = NZ // BLOCK_PLANES

    def one_block(block_index):
        window = lax.dynamic_slice_in_dim(padded, block_index * BLOCK_PLANES, BLOCK_PLANES + 2, 1)
        return tendency_block(window)
    tendency = lax.map(one_block, jnp.arange(block_count, dtype=jnp.int32))
    tendency = jnp.moveaxis(tendency, 0, 1).reshape(5, NZ, NX, NY)
    section_next = 0.75 * section_start + 0.25 * (section_now + TIME_STEP * tendency)
    sample = section_next[:, ::ZSUB]
    snapshot = pressure_of(sample).astype(jnp.bfloat16)

    def add_block(running, block_index):
        older = lax.dynamic_slice_in_dim(history, block_index * CX, CX, 2).reshape(SNAPS - 1, -1)
        newest = lax.dynamic_slice_in_dim(snapshot, block_index * CX, CX, 1).reshape(1, -1)
        matrix = jnp.concatenate([older, newest], axis=0)
        product = lax.dot_general(matrix.astype(jnp.float32), matrix.astype(jnp.float32), (((1,), (1,)), ((), ())), preferred_element_type=jnp.float32)
        return (running + product, None)
    gram_total, _ = lax.scan(add_block, jnp.zeros((SNAPS, SNAPS), jnp.float32), jnp.arange(N_GX, dtype=jnp.int32))
    rows_total = NZ // ZSUB * NX * NY
    triangle = jnp.linalg.cholesky(gram_total / rows_total).T
    return (section_next, triangle)
```

```python
import functools

import jax
import jax.numpy as jnp
from jax import lax
from jax.experimental import pallas as pl
from jax.experimental.pallas import tpu as pltpu
from jax.sharding import PartitionSpec as P

ZSUB = 4
GAMMA_LESS = 0.4
TIME_STEP = 0.2
VISCOUS = 0.25
MESH = pl.DeviceIdType.MESH
FLUX = 0.25 * TIME_STEP * 0.5
NEAR = 0.25 * TIME_STEP * VISCOUS
OWN = 0.25 - 6.0 * NEAR


def wait_bytes(ref, sem):
    pltpu.make_async_copy(ref, ref, sem).wait()


def pressure_of(q, inverse):
    kinetic = q[1] * q[1] + q[2] * q[2] + q[3] * q[3]
    return GAMMA_LESS * (q[4] - 0.5 * kinetic * inverse)


def plane_of(q):
    inverse = 1.0 / q[0]
    pressure = pressure_of(q, inverse)
    return q, inverse * FLUX, pressure * FLUX, q[4] + pressure


def flux_of(plane, k, sign=None):
    q, scaled, pressure, enthalpy = plane
    if sign is not None:
        scaled, pressure = scaled * sign, pressure * sign
    velocity = q[k] * scaled
    flux = [q[0] * velocity]
    for member in (1, 2, 3):
        term = q[member] * velocity
        flux.append(term + pressure if member == k else term)
    flux.append(enthalpy * velocity)
    return flux


def both_of(plane, k):
    flux = flux_of(plane, k)
    base = [NEAR * value for value in plane[0]]
    return [b + f for b, f in zip(base, flux)], [b - f for b, f in zip(base, flux)]


def edge_of(q, k, sign):
    flux = flux_of(plane_of(q), k, sign)
    return [NEAR * value + f for value, f in zip(q, flux)]


def fold(acc, first, second):
    row = lax.broadcasted_iota(jnp.int32, (256, 128), 0)
    col = lax.broadcasted_iota(jnp.int32, (256, 128), 1)
    total = jnp.zeros((128, 128), jnp.float32)
    for parity in (0, 1):
        pick = (row == 2 * col + parity).astype(jnp.bfloat16)
        for h in (0, 1):
            part = acc[2 * second + h, pl.ds(256 * first + parity, 128, stride=2), :]
            chosen = pick[128 * h : 128 * h + 128]
            for piece in split_of(part):
                total = total + jnp.dot(piece, chosen, preferred_element_type=jnp.float32)
    return total


def split_of(x):
    high = x.astype(jnp.bfloat16)
    rest = x - high.astype(jnp.float32)
    middle = rest.astype(jnp.bfloat16)
    low = (rest - middle.astype(jnp.float32)).astype(jnp.bfloat16)
    return high, middle, low


def section_kernel(
    n_gx, n_gy, planes,
    rows_hbm, now_hbm, start_hbm, hist_hbm, next_hbm, gram_out,
    now, start, result, hist, acc, xhalo, ysend, yhalo,
    packed, rs, rs_extra, ex, gat,
    now_sem, start_sem, hist_sem, out_sem,
    xs, xr, ys, yr, rs_s, rs_r, re_s, re_r, ex_s, ex_r, ag_s, ag_r, ae_s, ae_r,
):
    a, c = lax.axis_index("gx"), lax.axis_index("gy")
    samples = planes // ZSUB
    pairs = hist_hbm.shape[1] // samples
    older = hist_hbm.shape[0]
    load_now = pltpu.make_async_copy(now_hbm, now, now_sem)
    load_start = pltpu.make_async_copy(start_hbm, start, start_sem)
    load_now.start()
    barrier = pltpu.get_barrier_semaphore()

    def greet_gx(d, carry):
        pl.semaphore_signal(barrier, inc=1, device_id=(lax.rem(a + d, n_gx), c), device_id_type=MESH)
        return carry

    def greet_gy(d, carry):
        pl.semaphore_signal(barrier, inc=1, device_id=(a, lax.rem(c + d, n_gy)), device_id_type=MESH)
        return carry

    lax.fori_loop(1, n_gx, greet_gx, 0)
    lax.fori_loop(1, n_gy, greet_gy, 0)
    load_start.start()

    def load_history(z, carry):
        for i in range(pairs):
            pltpu.make_async_copy(
                hist_hbm.at[:, z * pairs + i], hist.at[z * pairs + i, pl.ds(0, older)], hist_sem.at[z]
            ).start()
        return carry

    lax.fori_loop(0, samples, load_history, 0)

    lane = lax.broadcasted_iota(jnp.int32, (8, 128), 1)
    sub = lax.broadcasted_iota(jnp.int32, (8, 128), 0)
    load_now.wait()

    def pack_edges(z, carry):
        mask = lax.rem(lane - 2 * z + 129, 128) < 2
        return tuple(
            jnp.where(mask, pltpu.roll(now[f, z], 2 * z, 1), carry[f]) for f in range(5)
        )

    zero = jnp.zeros((8, 128), jnp.float32)
    edges = lax.fori_loop(0, planes, pack_edges, (zero,) * 5, unroll=4)
    for f in range(5):
        ysend[f] = edges[f]

    pl.semaphore_wait(barrier, n_gx + n_gy - 2)
    up, down = lax.rem(a + 1, n_gx), lax.rem(a + n_gx - 1, n_gx)
    ahead, behind = lax.rem(c + 1, n_gy), lax.rem(c + n_gy - 1, n_gy)

    def to(src, dst, send, recv, where):
        return pltpu.make_async_remote_copy(
            src_ref=src, dst_ref=dst, send_sem=send, recv_sem=recv, device_id=where, device_id_type=MESH
        )

    halos = [
        to(ysend, yhalo.at[0], ys.at[0], yr.at[0], (a, ahead)),
        to(ysend, yhalo.at[1], ys.at[1], yr.at[1], (a, behind)),
        to(rows_hbm.at[:, :, 7], xhalo.at[0], xs.at[0], xr.at[0], (up, c)),
        to(rows_hbm.at[:, :, 0], xhalo.at[1], xs.at[1], xr.at[1], (down, c)),
    ]
    for copy in halos:
        copy.start()
    acc[...] = jnp.zeros_like(acc)
    load_start.wait()
    for copy in halos:
        copy.wait()
    even = lax.rem(lane, 2) == 0
    for f in range(5):
        ysend[f] = jnp.where(even, yhalo[1, f], yhalo[0, f])
    xsign = jnp.where(sub == 7, 1.0, -1.0)
    ysign = jnp.where(lane == 127, 1.0, -1.0)

    def load(z):
        return plane_of([now[f, z] for f in range(5)])

    first = both_of(load(0), 3)[0]

    def step(s, carry):
        below, here = list(carry[:5]), list(carry[5:])
        z0 = s * ZSUB
        plane = load(z0)
        for k in range(ZSUB):
            z = z0 + k
            above = load(jnp.minimum(z + 1, planes - 1))
            up3, down3 = both_of(above, 3)
            p1, n1 = both_of(plane, 1)
            p2, n2 = both_of(plane, 2)
            xq = [jnp.where(sub < 4, xhalo[1, f, z], xhalo[0, f, z]) for f in range(5)]
            xe = edge_of(xq, 1, xsign)
            turn = lax.rem(128 - 2 * z, 128)
            yq = [pltpu.roll(ysend[f], turn, 1) for f in range(5)]
            yq[0] = jnp.where((lane == 0) | (lane == 127), yq[0], 1.0)
            ye = edge_of(yq, 2, ysign)
            fresh = []
            for f in range(5):
                total = below[f] + down3[f]
                total += pltpu.roll(jnp.where(sub == 7, xe[f], p1[f]), 1, 0)
                total += pltpu.roll(jnp.where(sub == 0, xe[f], n1[f]), 7, 0)
                total += pltpu.roll(jnp.where(lane == 127, ye[f], p2[f]), 1, 1)
                total += pltpu.roll(jnp.where(lane == 0, ye[f], n2[f]), 127, 1)
                total += 0.75 * start[f, z] + OWN * plane[0][f]
                result[f, z] = total
                fresh.append(total)
            below, here, plane = here, up3, above
            if k == 0:
                snapshot = pressure_of(fresh, 1.0 / fresh[0]).astype(jnp.bfloat16)
                spot = pl.multiple_of(s * pairs, pairs)
                wait_bytes(hist.at[pl.ds(spot, pairs), pl.ds(0, older)], hist_sem.at[s])
                hist[pl.ds(spot, pairs), older] = snapshot.reshape(pairs, 2, 128)
                block = jnp.concatenate(
                    [hist[spot + i].reshape(2 * older + 2, 128) for i in range(pairs)], axis=1
                )
                for i, j in ((0, 0), (0, 1), (1, 1)):
                    rows, cols = slice(256 * i, 256 * i + 256), slice(256 * j, 256 * j + 256)
                    product = lax.dot_general(
                        block[rows], block[cols], (((1,), (1,)), ((), ())),
                        preferred_element_type=jnp.float32,
                    )
                    acc[2 * j, rows] += product[:, :128]
                    acc[2 * j + 1, rows] += product[:, 128:]
        pltpu.make_async_copy(
            result.at[:, pl.ds(z0, ZSUB)], next_hbm.at[:, pl.ds(z0, ZSUB)], out_sem
        ).start()
        return tuple(below + here)

    lax.fori_loop(0, samples, step, tuple(first + first))

    g00, g01, g11 = fold(acc, 0, 0), fold(acc, 0, 1), fold(acc, 1, 1)
    row = lax.broadcasted_iota(jnp.int32, (128, 128), 0)
    col = lax.broadcasted_iota(jnp.int32, (128, 128), 1)
    mixed = jnp.where(col >= row, g00, g11)
    diagonal = jnp.sum(jnp.where(col == row, g11, 0.0), axis=0, keepdims=True)
    for t in range(16):
        packed[t] = mixed[8 * t : 8 * t + 8]
        packed[16 + t] = g01[8 * t : 8 * t + 8]
    packed[32] = jnp.broadcast_to(diagonal, (8, 128))

    def scatter(d, carry):
        far = lax.rem(a + d, n_gx)
        to(packed.at[far], rs.at[a], rs_s, rs_r, (far, c)).start()
        return carry

    @pl.when(a != 0)
    def _():
        to(packed.at[32], rs_extra.at[a], re_s, re_r, (0, c)).start()

    lax.fori_loop(1, n_gx, scatter, 0)
    rs[a] = packed[a]
    others = pl.ds(0, n_gx - 1)
    wait_bytes(rs.at[others], rs_r)

    def total_of(ref, count):
        total = ref[0]
        for i in range(1, count):
            total = total + ref[i]
        return total

    ex[c, 0] = total_of(rs, n_gx)
    ex[c, 1] = zero

    @pl.when(a == 0)
    def _():
        rs_extra[0] = packed[32]
        wait_bytes(rs_extra.at[others], re_r)
        ex[c, 1] = total_of(rs_extra, n_gx)

    def exchange(d, carry):
        near = lax.rem(c + d, n_gy)
        to(ex.at[c], ex.at[c], ex_s, ex_r, (a, near)).start()
        return carry

    lax.fori_loop(1, n_gy, exchange, 0)
    wait_bytes(ex.at[pl.ds(0, n_gy - 1)], ex_r)
    whole = total_of(ex, n_gy)
    gat[a] = whole[0]

    def spread(d, carry):
        far = lax.rem(a + d, n_gx)
        to(gat.at[a], gat.at[a], ag_s, ag_r, (far, c)).start()
        return carry

    lax.fori_loop(1, n_gx, spread, 0)

    @pl.when(a == 0)
    def _():
        gat[32] = whole[1]

        def spread_extra(d, carry):
            to(gat.at[32], gat.at[32], ae_s, ae_r, (d, c)).start()
            return carry

        lax.fori_loop(1, n_gx, spread_extra, 0)

    wait_bytes(gat.at[others], ag_r)

    @pl.when(a != 0)
    def _():
        wait_bytes(gat.at[32], ae_r)
        wait_bytes(packed.at[32], re_s)

    @pl.when(a == 0)
    def _():
        wait_bytes(gat.at[others], ae_s)

    wait_bytes(rs.at[others], rs_s)
    wait_bytes(ex.at[pl.ds(0, n_gy - 1)], ex_s)
    wait_bytes(gat.at[others], ag_s)
    gram_out[...] = gat[...]
    wait_bytes(result, out_sem)


def factor(u, out):
    sub = lax.broadcasted_iota(jnp.int32, (8, 128), 0)
    lane = lax.broadcasted_iota(jnp.int32, (8, 128), 1)
    zero = jnp.zeros((8, 128), jnp.float32)
    for b in range(32):
        r0 = 8 * b
        half, off = r0 // 128, r0 % 128
        halves = [0, 1] if half == 0 else [1]
        panel = {h: u[r0 : r0 + 8, 128 * h : 128 * h + 128] for h in halves}
        cols = [jnp.broadcast_to(panel[half][:, off + j : off + j + 1], (8, 128)) for j in range(8)]
        d = {
            (i, j): jnp.broadcast_to(cols[j][i : i + 1, :], (8, 128))
            for j in range(8)
            for i in range(j + 1)
        }
        rows = {h: [jnp.broadcast_to(panel[h][i : i + 1, :], (8, 128)) for i in range(8)] for h in halves}
        last = b == 31
        if not last:
            n0 = r0 + 8
            nhalf = n0 // 128
            nh = [0, 1] if nhalf == 0 else [1]
            following = {h: u[n0 : n0 + 8, 128 * h : 128 * h + 128] for h in nh}
            src = u[n0 : n0 + 8, 128 * half : 128 * half + 128]
            g = [jnp.broadcast_to(src[:, off + j : off + j + 1], (8, 128)) for j in range(8)]
        for j in range(8):
            scale = lax.rsqrt(d[j, j])
            for k in range(j + 1, 8):
                d[j, k] = d[j, k] * scale
            for h in halves:
                rows[h][j] = rows[h][j] * scale
            if not last:
                g[j] = g[j] * scale
                for h in nh:
                    following[h] = following[h] - g[j] * rows[h][j]
            for k in range(j + 1, 8):
                for l in range(k, 8):
                    d[k, l] = d[k, l] - d[j, k] * d[j, l]
                for h in halves:
                    rows[h][k] = rows[h][k] - d[j, k] * rows[h][j]
                if not last:
                    g[k] = g[k] - d[j, k] * g[j]
        done = {}
        for h in halves:
            x = rows[h][7]
            for i in range(7):
                x = jnp.where(sub == i, rows[h][i], x)
            done[h] = x
        for h in (0, 1):
            if h < half:
                value = zero
            elif h == half:
                value = jnp.where(lane >= off + sub, done[h], 0.0)
            else:
                value = done[h]
            out[r0 : r0 + 8, 128 * h : 128 * h + 128] = value
        if last:
            break
        for h in nh:
            u[n0 : n0 + 8, 128 * h : 128 * h + 128] = following[h]
        t0 = n0 + 8
        if t0 < 256:
            hs = [h for h in halves if h >= nhalf]
            parts = {h: split_of(done[h]) for h in hs}
            c0 = 128 * nhalf

            def stack(order):
                return jnp.concatenate(
                    [jnp.concatenate([parts[h][o] for h in hs], axis=1) for o in order], axis=0
                )

            left, right = stack([0, 0, 1, 1, 0, 2]), stack([0, 1, 0, 1, 2, 0])
            product = lax.dot_general(
                left[:, t0 - c0 :], right, (((0,), (0,)), ((), ())), preferred_element_type=jnp.float32
            )
            u[t0:256, c0:256] = u[t0:256, c0:256] - product


def factor_kernel(scale, gram, temp_hbm, next_hbm, triangle, u, sem):
    move = pltpu.make_async_copy(temp_hbm, next_hbm, sem)
    move.start()
    row = lax.broadcasted_iota(jnp.int32, (128, 128), 0)
    col = lax.broadcasted_iota(jnp.int32, (128, 128), 1)
    mixed = gram[0:16].reshape(128, 128) * scale
    cross = gram[16:32].reshape(128, 128) * scale
    diagonal = jnp.broadcast_to(gram[32, 0:1] * scale, (128, 128))
    turned = mixed.T
    u[0:128, 0:128] = jnp.where(col >= row, mixed, turned)
    u[128:256, 128:256] = jnp.where(col == row, diagonal, jnp.where(col < row, mixed, turned))
    u[0:128, 128:256] = cross
    u[128:256, 0:128] = cross.T
    factor(u, triangle)
    move.wait()


def local(n_gx, n_gy, section_start, section_now, history):
    fields, planes, cx, cy = section_now.shape
    older, samples = history.shape[:2]
    f32, bf16 = jnp.float32, jnp.bfloat16
    any_space = pl.BlockSpec(memory_space=pl.ANY)
    vmem = pl.BlockSpec(memory_space=pltpu.VMEM)
    section = jax.ShapeDtypeStruct(section_now.shape, f32)
    dma = pltpu.SemaphoreType.DMA
    tiles = n_gx + 1
    temp, gram = pl.pallas_call(
        functools.partial(section_kernel, n_gx, n_gy, planes),
        out_shape=(section, jax.ShapeDtypeStruct((tiles, 8, 128), f32)),
        in_specs=[any_space] * 4,
        out_specs=(any_space, vmem),
        scratch_shapes=[
            pltpu.VMEM(section_now.shape, f32),
            pltpu.VMEM(section_now.shape, f32),
            pltpu.VMEM(section_now.shape, f32),
            pltpu.VMEM((samples * cx // 2, older + 1, 2, cy), bf16),
            pltpu.VMEM((4, 2 * older + 2, 128), f32),
            pltpu.VMEM((2, fields, planes, 1, cy), f32),
            pltpu.VMEM((fields, cx, cy), f32),
            pltpu.VMEM((2, fields, cx, cy), f32),
            pltpu.VMEM((tiles, 8, 128), f32),
            pltpu.VMEM((n_gx, 8, 128), f32),
            pltpu.VMEM((n_gx, 8, 128), f32),
            pltpu.VMEM((n_gy, 2, 8, 128), f32),
            pltpu.VMEM((tiles, 8, 128), f32),
            dma, dma, dma((samples,)), dma,
            dma((2,)), dma((2,)), dma((2,)), dma((2,)),
        ] + [dma] * 10,
        compiler_params=pltpu.CompilerParams(
            collective_id=0, has_side_effects=True, vmem_limit_bytes=40 << 20
        ),
    )(
        section_now.reshape(fields, planes, cx, 1, cy),
        section_now,
        section_start,
        history.reshape(older, samples * cx // 2, 2, cy),
    )
    rows = samples * cx * cy * n_gx * n_gy
    return pl.pallas_call(
        functools.partial(factor_kernel, 1.0 / rows),
        out_shape=(section, jax.ShapeDtypeStruct((older + 1, older + 1), f32)),
        in_specs=[vmem, any_space],
        out_specs=(any_space, vmem),
        scratch_shapes=[pltpu.VMEM((older + 1, older + 1), f32), dma],
    )(gram, temp)


def solution(mesh):
    spec = P(None, None, "gx", "gy")
    return jax.shard_map(
        functools.partial(local, mesh.shape["gx"], mesh.shape["gy"]),
        mesh=mesh,
        in_specs=(spec, spec, spec),
        out_specs=(spec, P()),
        check_vma=False,
    )
```

```python
import functools

import jax
import jax.numpy as jnp
from jax import lax
from jax.experimental import pallas as pl
from jax.experimental.pallas import tpu as pltpu
from jax.sharding import PartitionSpec as P

ZSUB = 4
LINE = 4
EARLY = 8
CUTS = (6, 10)
GAMMA_LESS = 0.4
TIME_STEP = 0.2
VISCOUS = 0.25
MESH = pl.DeviceIdType.MESH
FLUX = 0.25 * TIME_STEP * 0.5
NEAR = 0.25 * TIME_STEP * VISCOUS
OWN = 0.25 - 6.0 * NEAR


def wait_bytes(ref, sem):
    pltpu.make_async_copy(ref, ref, sem).wait()


def pressure_of(q, inverse):
    kinetic = q[1] * q[1] + q[2] * q[2] + q[3] * q[3]
    return GAMMA_LESS * (q[4] - 0.5 * kinetic * inverse)


def plane_of(q):
    inverse = 1.0 / q[0]
    pressure = pressure_of(q, inverse)
    return q, inverse * FLUX, pressure * FLUX, q[4] + pressure


def flux_of(plane, k, sign=None):
    q, scaled, pressure, enthalpy = plane
    if sign is not None:
        scaled, pressure = scaled * sign, pressure * sign
    velocity = q[k] * scaled
    flux = [q[0] * velocity]
    for member in (1, 2, 3):
        term = q[member] * velocity
        flux.append(term + pressure if member == k else term)
    flux.append(enthalpy * velocity)
    return flux


def both_of(plane, k):
    flux = flux_of(plane, k)
    base = [NEAR * value for value in plane[0]]
    return [b + f for b, f in zip(base, flux)], [b - f for b, f in zip(base, flux)]


def edge_of(q, k, sign):
    flux = flux_of(plane_of(q), k, sign)
    return [NEAR * value + f for value, f in zip(q, flux)]


def fold(acc, first, second):
    row = lax.broadcasted_iota(jnp.int32, (256, 128), 0)
    col = lax.broadcasted_iota(jnp.int32, (256, 128), 1)
    total = jnp.zeros((128, 128), jnp.float32)
    for parity in (0, 1):
        pick = (row == 2 * col + parity).astype(jnp.bfloat16)
        for h in (0, 1):
            part = acc[2 * second + h, pl.ds(256 * first + parity, 128, stride=2), :]
            chosen = pick[128 * h : 128 * h + 128]
            for piece in split_of(part):
                total = total + jnp.dot(piece, chosen, preferred_element_type=jnp.float32)
    return total


def split_of(x):
    high = x.astype(jnp.bfloat16)
    rest = x - high.astype(jnp.float32)
    middle = rest.astype(jnp.bfloat16)
    low = (rest - middle.astype(jnp.float32)).astype(jnp.bfloat16)
    return high, middle, low


def section_kernel(
    n_gx, n_gy, planes,
    rows_hbm, now_hbm, start_hbm, hist_hbm, next_hbm, gram_out,
    now, start, result, hist, acc, acc_new, xhalo, xrest, ysend, yhalo, yedge,
    packed, rs, rs_extra, ex, gat,
    now_sem, start_sem, hist_sem, out_sem,
    xs, xr, ys, yr, rs_s, rs_r, re_s, re_r, ex_s, ex_r, ag_s, ag_r, ae_s, ae_r,
):
    a, c = lax.axis_index("gx"), lax.axis_index("gy")
    n_z = n_gx // LINE
    zz, yy = a // LINE, lax.rem(a, LINE)
    n_near = LINE * n_gy
    me = yy * n_gy + c
    samples = planes // ZSUB
    pairs = hist_hbm.shape[1] // samples
    older = hist_hbm.shape[0]
    load_now = pltpu.make_async_copy(now_hbm, now, now_sem)
    load_start = pltpu.make_async_copy(start_hbm, start, start_sem)
    load_now.start()
    barrier = pltpu.get_barrier_semaphore()
    up, down = lax.rem(a + 1, n_gx), lax.rem(a + n_gx - 1, n_gx)
    ahead, behind = lax.rem(c + 1, n_gy), lax.rem(c + n_gy - 1, n_gy)

    def near_of(d):
        order = lax.rem(d, LINE)
        turn = d // LINE
        dy = jnp.where(order == 0, 2, jnp.where(order == 3, 0, 2 * order - 1))
        other = n_gy - 1 - turn
        dc = jnp.where(other < 2, other, jnp.where(other < 4, other + 4, other - 2))
        y = lax.rem(yy + dy, LINE)
        return y, lax.rem(c + dc, n_gy)

    def far_of(d):
        half = n_z // 2
        dz = jnp.where(lax.rem(d, 2) == 0, half + d // 2, half - 1 - d // 2)
        return lax.rem(zz + dz, n_z)

    def greet(where):
        pl.semaphore_signal(barrier, inc=1, device_id=where, device_id_type=MESH)

    def greet_near(d, carry):
        y, core = near_of(d)
        greet((zz * LINE + y, core))
        return carry

    def greet_far(d, carry):
        greet((far_of(d) * LINE + yy, c))
        return carry

    for where in ((up, c), (down, c), (a, ahead), (a, behind)):
        greet(where)
    lax.fori_loop(0, n_near - 1, greet_near, 0)
    lax.fori_loop(0, n_z - 1, greet_far, 0)

    def load_history(z, carry):
        for i in range(pairs):
            pltpu.make_async_copy(
                hist_hbm.at[:, z * pairs + i], hist.at[z * pairs + i, pl.ds(0, older)], hist_sem.at[z]
            ).start()
        return carry

    lax.fori_loop(0, samples // 2, load_history, 0)
    load_start.start()
    pl.semaphore_wait(barrier, n_near - 1 + n_z - 1 + 4)

    def to(src, dst, send, recv, where):
        return pltpu.make_async_remote_copy(
            src_ref=src, dst_ref=dst, send_sem=send, recv_sem=recv, device_id=where, device_id_type=MESH
        )

    halos = [
        to(rows_hbm.at[:, :, 0, 7], xhalo.at[0], xs.at[0], xr.at[0], (up, c)),
        to(rows_hbm.at[:, :, 0, 0], xhalo.at[1], xs.at[1], xr.at[1], (down, c)),
        to(ysend.at[0], yhalo.at[0, 0], ys.at[0], yr.at[0], (a, ahead)),
        to(ysend.at[0], yhalo.at[0, 1], ys.at[1], yr.at[1], (a, behind)),
    ]
    rest = [
        to(rows_hbm.at[:, :, pl.ds(1, ZSUB - 1), 7], xrest.at[0], xs.at[2], xr.at[2], (up, c)),
        to(rows_hbm.at[:, :, pl.ds(1, ZSUB - 1), 0], xrest.at[1], xs.at[3], xr.at[3], (down, c)),
        to(ysend.at[1], yhalo.at[1, 0], ys.at[2], yr.at[2], (a, ahead)),
        to(ysend.at[1], yhalo.at[1, 1], ys.at[3], yr.at[3], (a, behind)),
    ]
    halos[0].start()
    halos[1].start()
    lane = lax.broadcasted_iota(jnp.int32, (8, 128), 1)
    sub = lax.broadcasted_iota(jnp.int32, (8, 128), 0)
    zero = jnp.zeros((8, 128), jnp.float32)
    load_now.wait()

    def pack_edges(count, stride, where):
        def one(i, carry):
            mask = lax.rem(lane - 2 * i + 129, 128) < 2
            return tuple(
                jnp.where(mask, pltpu.roll(now[f, i * stride], 2 * i, 1), carry[f]) for f in range(5)
            )

        edges = lax.fori_loop(0, count, one, (zero,) * 5, unroll=4)
        for f in range(5):
            ysend[where, f] = edges[f]

    pack_edges(samples, ZSUB, 0)
    halos[2].start()
    halos[3].start()
    rest[0].start()
    rest[1].start()
    lax.fori_loop(samples // 2, samples, load_history, 0)
    pack_edges(planes, 1, 1)
    rest[2].start()
    rest[3].start()

    acc[...] = jnp.zeros_like(acc)
    acc_new[...] = jnp.zeros_like(acc_new)
    hist[pl.ds(0, EARLY * pairs), older] = jnp.zeros((EARLY * pairs, 2, 128), jnp.bfloat16)

    def block_of(s):
        return jnp.concatenate(
            [hist[s * pairs + i].reshape(2 * older + 2, 128) for i in range(pairs)], axis=1
        )

    def multiply(s):
        block = block_of(s)
        for i, j in ((0, 0), (0, 1), (1, 1)):
            rows, cols = slice(256 * i, 256 * i + 256), slice(256 * j, 256 * j + 256)
            product = lax.dot_general(
                block[rows], block[cols], (((1,), (1,)), ((), ())), preferred_element_type=jnp.float32
            )
            acc[2 * j, rows] += product[:, :128]
            acc[2 * j + 1, rows] += product[:, 128:]

    def wait_history(s):
        spot = pl.multiple_of(s * pairs, pairs)
        wait_bytes(hist.at[pl.ds(spot, pairs), pl.ds(0, older)], hist_sem.at[s])

    def early(s, carry):
        wait_history(s)
        multiply(s)
        return carry

    lax.fori_loop(0, EARLY, early, 0)
    load_start.wait()
    for copy in halos:
        copy.wait_recv()
    even = lax.rem(lane, 2) == 0

    def merge_edges(which):
        for f in range(5):
            yedge[which, f] = jnp.where(even, yhalo[which, 1, f], yhalo[which, 0, f])

    merge_edges(0)
    xsign = jnp.where(sub == 7, 1.0, -1.0)
    ysign = jnp.where(lane == 127, 1.0, -1.0)

    def load(z):
        return plane_of([now[f, z] for f in range(5)])

    def advance(z, plane, below, above, low, high, which, i):
        p1, n1 = both_of(plane, 1)
        p2, n2 = both_of(plane, 2)
        xe = edge_of([jnp.where(sub < 4, high[f], low[f]) for f in range(5)], 1, xsign)
        turn = lax.rem(128 - 2 * i, 128)
        yq = [pltpu.roll(yedge[which, f], turn, 1) for f in range(5)]
        yq[0] = jnp.where((lane == 0) | (lane == 127), yq[0], 1.0)
        ye = edge_of(yq, 2, ysign)
        fresh = []
        for f in range(5):
            total = below[f] + above[f]
            total += pltpu.roll(jnp.where(sub == 7, xe[f], p1[f]), 1, 0)
            total += pltpu.roll(jnp.where(sub == 0, xe[f], n1[f]), 7, 0)
            total += pltpu.roll(jnp.where(lane == 127, ye[f], p2[f]), 1, 1)
            total += pltpu.roll(jnp.where(lane == 0, ye[f], n2[f]), 127, 1)
            total += 0.75 * start[f, z] + OWN * plane[0][f]
            result[f, z] = total
            fresh.append(total)
        return fresh

    def sampled(s):
        z = s * ZSUB
        below = both_of(load(jnp.maximum(z - 1, 0)), 3)[0]
        above = both_of(load(z + 1), 3)[1]
        low, high = ([xhalo[side, f, s] for f in range(5)] for side in (0, 1))
        fresh = advance(z, load(z), below, above, low, high, 0, s)
        snapshot = pressure_of(fresh, 1.0 / fresh[0]).astype(jnp.bfloat16)
        hist[pl.ds(pl.multiple_of(s * pairs, pairs), pairs), older] = snapshot.reshape(pairs, 2, 128)

    def sample_two(i, carry):
        sampled(2 * i)
        sampled(2 * i + 1)
        return carry

    def late(s, carry):
        wait_history(s)
        multiply(s)
        return carry

    def newest(s, carry):
        block = block_of(s)
        acc_new[:, 0:16] += lax.dot_general(
            block, block[2 * older - 14 :], (((1,), (1,)), ((), ())), preferred_element_type=jnp.float32
        )
        return carry

    lax.fori_loop(0, samples // 2, sample_two, 0)
    lax.fori_loop(0, EARLY, newest, 0)
    lax.fori_loop(EARLY, samples, late, 0)

    row = lax.broadcasted_iota(jnp.int32, (128, 128), 0)
    col = lax.broadcasted_iota(jnp.int32, (128, 128), 1)

    def added(first):
        total = jnp.zeros((128, 128), jnp.float32)
        for parity in (0, 1):
            part = acc_new[pl.ds(256 * first + parity, 128, stride=2), :]
            total += jnp.broadcast_to(part[:, 14 + parity : 15 + parity], (128, 128))
        return jnp.where(col == 127, total, 0.0)

    g00 = fold(acc, 0, 0)
    g01 = fold(acc, 0, 1) + added(0)
    g11 = fold(acc, 1, 1) + added(1)
    mixed = jnp.where(col >= row, g11, g00)
    diagonal = jnp.sum(jnp.where(col == row, g00, 0.0), axis=0, keepdims=True)
    for t in range(16):
        packed[t] = mixed[8 * t : 8 * t + 8]
        packed[16 + t] = g01[8 * t : 8 * t + 8]
    packed[n_near] = jnp.broadcast_to(diagonal, (8, 128))

    def scatter(d, carry):
        y, core = near_of(d)
        to(packed.at[y * n_gy + core], rs.at[me], rs_s, rs_r, (zz * LINE + y, core)).start()
        return carry

    @pl.when(me != 0)
    def _():
        to(packed.at[n_near], rs_extra.at[me], re_s, re_r, (zz * LINE, 0)).start()

    lax.fori_loop(0, n_near - 1, scatter, 0, unroll=True)
    rs[me] = packed[me]
    for copy in rest:
        copy.wait_recv()
    merge_edges(1)

    def others(s, carry):
        z0 = s * ZSUB
        parts = [load(z0)]
        below = both_of(parts[0], 3)[0]
        here = load(z0 + 1)
        for k in range(1, ZSUB):
            z = z0 + k
            above = load(jnp.minimum(z + 1, planes - 1))
            low, high = ([xrest[side, f, s, k - 1] for f in range(5)] for side in (0, 1))
            advance(z, here, below, both_of(above, 3)[1], low, high, 1, z)
            below, here = both_of(here, 3)[0], above
        return carry

    def finish(first, last):
        lax.fori_loop(first, last, others, 0)
        part = pl.ds(first * ZSUB, (last - first) * ZSUB)
        pltpu.make_async_copy(result.at[:, part], next_hbm.at[:, part], out_sem).start()

    finish(0, CUTS[0])
    near_rest, far_rest = pl.ds(0, n_near - 1), pl.ds(0, n_z - 1)
    wait_bytes(rs.at[near_rest], rs_r)

    def total_of(ref, count):
        parts = [ref[i] for i in range(count)]
        while len(parts) > 1:
            parts = [sum(parts[i : i + 2]) for i in range(0, len(parts), 2)]
        return parts[0]

    ex[zz, 0] = total_of(rs, n_near)
    ex[zz, 1] = zero

    @pl.when(me == 0)
    def _():
        rs_extra[0] = packed[n_near]
        wait_bytes(rs_extra.at[near_rest], re_r)
        ex[zz, 1] = total_of(rs_extra, n_near)

    def exchange(d, carry):
        to(ex.at[zz], ex.at[zz], ex_s, ex_r, (far_of(d) * LINE + yy, c)).start()
        return carry

    lax.fori_loop(0, n_z - 1, exchange, 0, unroll=True)
    finish(CUTS[0], CUTS[1])
    wait_bytes(ex.at[far_rest], ex_r)
    whole = total_of(ex, n_z)
    gat[me] = whole[0]

    def spread(d, carry):
        y, core = near_of(d)
        to(gat.at[me], gat.at[me], ag_s, ag_r, (zz * LINE + y, core)).start()
        return carry

    @pl.when(me == 0)
    def _():
        gat[n_near] = whole[1]

        def spread_extra(d, carry):
            y, core = near_of(d)
            to(gat.at[n_near], gat.at[n_near], ae_s, ae_r, (zz * LINE + y, core)).start()
            return carry

        lax.fori_loop(0, n_near - 1, spread_extra, 0)

    lax.fori_loop(0, n_near - 1, spread, 0, unroll=True)
    finish(CUTS[1], samples)
    wait_bytes(gat.at[near_rest], ag_r)

    @pl.when(me != 0)
    def _():
        wait_bytes(gat.at[n_near], ae_r)
        wait_bytes(packed.at[n_near], re_s)

    @pl.when(me == 0)
    def _():
        wait_bytes(gat.at[near_rest], ae_s)

    gram_out[...] = gat[...]
    wait_bytes(rs.at[near_rest], rs_s)
    wait_bytes(ex.at[far_rest], ex_s)
    wait_bytes(gat.at[near_rest], ag_s)
    for copy in halos + rest:
        copy.wait_send()
    wait_bytes(result, out_sem)


def factor(u, out):
    sub = lax.broadcasted_iota(jnp.int32, (8, 128), 0)
    lane = lax.broadcasted_iota(jnp.int32, (8, 128), 1)
    zero = jnp.zeros((8, 128), jnp.float32)
    for b in range(32):
        r0 = 8 * b
        half, off = r0 // 128, r0 % 128
        halves = [0, 1] if half == 0 else [1]
        panel = {h: u[r0 : r0 + 8, 128 * h : 128 * h + 128] for h in halves}
        cols = [jnp.broadcast_to(panel[half][:, off + j : off + j + 1], (8, 128)) for j in range(8)]
        d = {
            (i, j): jnp.broadcast_to(cols[j][i : i + 1, :], (8, 128))
            for j in range(8)
            for i in range(j + 1)
        }
        rows = {h: [jnp.broadcast_to(panel[h][i : i + 1, :], (8, 128)) for i in range(8)] for h in halves}
        last = b == 31
        if not last:
            n0 = r0 + 8
            nhalf = n0 // 128
            nh = [0, 1] if nhalf == 0 else [1]
            following = {h: u[n0 : n0 + 8, 128 * h : 128 * h + 128] for h in nh}
            src = u[n0 : n0 + 8, 128 * half : 128 * half + 128]
            g = [jnp.broadcast_to(src[:, off + j : off + j + 1], (8, 128)) for j in range(8)]
        for j in range(8):
            scale = lax.rsqrt(d[j, j])
            for k in range(j + 1, 8):
                d[j, k] = d[j, k] * scale
            for h in halves:
                rows[h][j] = rows[h][j] * scale
            if not last:
                g[j] = g[j] * scale
                for h in nh:
                    following[h] = following[h] - g[j] * rows[h][j]
            for k in range(j + 1, 8):
                for l in range(k, 8):
                    d[k, l] = d[k, l] - d[j, k] * d[j, l]
                for h in halves:
                    rows[h][k] = rows[h][k] - d[j, k] * rows[h][j]
                if not last:
                    g[k] = g[k] - d[j, k] * g[j]
        done = {}
        for h in halves:
            x = rows[h][7]
            for i in range(7):
                x = jnp.where(sub == i, rows[h][i], x)
            done[h] = x
        for h in (0, 1):
            if h < half:
                value = zero
            elif h == half:
                value = jnp.where(lane >= off + sub, done[h], 0.0)
            else:
                value = done[h]
            out[r0 : r0 + 8, 128 * h : 128 * h + 128] = value
        if last:
            break
        for h in nh:
            u[n0 : n0 + 8, 128 * h : 128 * h + 128] = following[h]
        t0 = n0 + 8
        if t0 < 256:
            hs = [h for h in halves if h >= nhalf]
            parts = {h: split_of(done[h]) for h in hs}
            c0 = 128 * nhalf

            def stack(order):
                return jnp.concatenate(
                    [jnp.concatenate([parts[h][o] for h in hs], axis=1) for o in order], axis=0
                )

            left, right = stack([0, 0, 1, 1, 0, 2]), stack([0, 1, 0, 1, 2, 0])
            product = lax.dot_general(
                left[:, t0 - c0 :], right, (((0,), (0,)), ((), ())), preferred_element_type=jnp.float32
            )
            u[t0:256, c0:256] = u[t0:256, c0:256] - product


def factor_kernel(scale, gram, temp_hbm, next_hbm, triangle, u, held, in_sem, out_sem):
    take = pltpu.make_async_copy(temp_hbm, held, in_sem)
    give = pltpu.make_async_copy(held, next_hbm, out_sem)
    take.start()
    row = lax.broadcasted_iota(jnp.int32, (128, 128), 0)
    col = lax.broadcasted_iota(jnp.int32, (128, 128), 1)
    mixed = gram[0:16].reshape(128, 128) * scale
    cross = gram[16:32].reshape(128, 128) * scale
    diagonal = jnp.broadcast_to(gram[32, 0:1] * scale, (128, 128))
    turned = mixed.T
    u[0:128, 0:128] = jnp.where(col == row, diagonal, jnp.where(col < row, mixed, turned))
    u[128:256, 128:256] = jnp.where(col >= row, mixed, turned)
    u[0:128, 128:256] = cross
    u[128:256, 0:128] = cross.T
    take.wait()
    give.start()
    factor(u, triangle)
    give.wait()


def local(n_gx, n_gy, section_start, section_now, history):
    fields, planes, cx, cy = section_now.shape
    older, samples = history.shape[:2]
    f32, bf16 = jnp.float32, jnp.bfloat16
    any_space = pl.BlockSpec(memory_space=pl.ANY)
    vmem = pl.BlockSpec(memory_space=pltpu.VMEM)
    section = jax.ShapeDtypeStruct(section_now.shape, f32)
    dma = pltpu.SemaphoreType.DMA
    tiles = n_gx + 1
    temp, gram = pl.pallas_call(
        functools.partial(section_kernel, n_gx, n_gy, planes),
        out_shape=(section, jax.ShapeDtypeStruct((tiles, 8, 128), f32)),
        in_specs=[any_space] * 4,
        out_specs=(any_space, vmem),
        scratch_shapes=[
            pltpu.VMEM(section_now.shape, f32),
            pltpu.VMEM(section_now.shape, f32),
            pltpu.VMEM(section_now.shape, f32),
            pltpu.VMEM((samples * cx // 2, older + 1, 2, cy), bf16),
            pltpu.VMEM((4, 2 * older + 2, 128), f32),
            pltpu.VMEM((2 * older + 2, 128), f32),
            pltpu.VMEM((2, fields, samples, 1, cy), f32),
            pltpu.VMEM((2, fields, samples, ZSUB - 1, 1, cy), f32),
            pltpu.VMEM((2, fields, cx, cy), f32),
            pltpu.VMEM((2, 2, fields, cx, cy), f32),
            pltpu.VMEM((2, fields, cx, cy), f32),
            pltpu.VMEM((tiles, 8, 128), f32),
            pltpu.VMEM((n_gx, 8, 128), f32),
            pltpu.VMEM((n_gx, 8, 128), f32),
            pltpu.VMEM((n_gx // LINE, 2, 8, 128), f32),
            pltpu.VMEM((tiles, 8, 128), f32),
            dma, dma, dma((samples,)), dma,
            dma((4,)), dma((4,)), dma((4,)), dma((4,)),
        ] + [dma] * 10,
        compiler_params=pltpu.CompilerParams(
            collective_id=0, has_side_effects=True, vmem_limit_bytes=60 << 20
        ),
    )(
        section_now.reshape(fields, samples, ZSUB, cx, 1, cy),
        section_now,
        section_start,
        history.reshape(older, samples * cx // 2, 2, cy),
    )
    rows = samples * cx * cy * n_gx * n_gy
    return pl.pallas_call(
        functools.partial(factor_kernel, 1.0 / rows),
        out_shape=(section, jax.ShapeDtypeStruct((older + 1, older + 1), f32)),
        in_specs=[vmem, any_space],
        out_specs=(any_space, vmem),
        scratch_shapes=[
            pltpu.VMEM((older + 1, older + 1), f32),
            pltpu.VMEM(section_now.shape, f32),
            dma, dma,
        ],
    )(gram, temp)


def solution(mesh):
    spec = P(None, None, "gx", "gy")
    return jax.shard_map(
        functools.partial(local, mesh.shape["gx"], mesh.shape["gy"]),
        mesh=mesh,
        in_specs=(spec, spec, spec),
        out_specs=(spec, P()),
        check_vma=False,
    )
```

```python
import functools

import jax
import jax.numpy as jnp
from jax import lax
from jax.experimental import pallas as pl
from jax.experimental.pallas import tpu as pltpu
from jax.sharding import PartitionSpec as P

ZSUB = 4
LINE = 4
GROUP = 4
AHEAD = 3
CUTS = (6, 10)
GAMMA_LESS = 0.4
TIME_STEP = 0.2
VISCOUS = 0.25
MESH = pl.DeviceIdType.MESH
FLUX = 0.25 * TIME_STEP * 0.5
NEAR = 0.25 * TIME_STEP * VISCOUS
OWN = 0.25 - 6.0 * NEAR


def wait_bytes(ref, sem):
    pltpu.make_async_copy(ref, ref, sem).wait()


def pressure_of(q, inverse):
    kinetic = q[1] * q[1] + q[2] * q[2] + q[3] * q[3]
    return GAMMA_LESS * (q[4] - 0.5 * kinetic * inverse)


def plane_of(q):
    inverse = 1.0 / q[0]
    pressure = pressure_of(q, inverse)
    return q, inverse * FLUX, pressure * FLUX, q[4] + pressure


def flux_of(plane, k, sign=None):
    q, scaled, pressure, enthalpy = plane
    if sign is not None:
        scaled, pressure = scaled * sign, pressure * sign
    velocity = q[k] * scaled
    flux = [q[0] * velocity]
    for member in (1, 2, 3):
        term = q[member] * velocity
        flux.append(term + pressure if member == k else term)
    flux.append(enthalpy * velocity)
    return flux


def both_of(plane, k):
    flux = flux_of(plane, k)
    base = [NEAR * value for value in plane[0]]
    return [b + f for b, f in zip(base, flux)], [b - f for b, f in zip(base, flux)]


def edge_of(q, k, sign):
    flux = flux_of(plane_of(q), k, sign)
    return [NEAR * value + f for value, f in zip(q, flux)]


def fold(acc, first, second):
    row = lax.broadcasted_iota(jnp.int32, (256, 128), 0)
    col = lax.broadcasted_iota(jnp.int32, (256, 128), 1)
    total = jnp.zeros((128, 128), jnp.float32)
    for parity in (0, 1):
        pick = (row == 2 * col + parity).astype(jnp.bfloat16)
        for h in (0, 1):
            part = acc[2 * second + h, pl.ds(256 * first + parity, 128, stride=2), :]
            chosen = pick[128 * h : 128 * h + 128]
            for piece in split_of(part):
                total = total + jnp.dot(piece, chosen, preferred_element_type=jnp.float32)
    return total


def split_of(x):
    high = x.astype(jnp.bfloat16)
    rest = x - high.astype(jnp.float32)
    middle = rest.astype(jnp.bfloat16)
    low = (rest - middle.astype(jnp.float32)).astype(jnp.bfloat16)
    return high, middle, low


def section_kernel(
    n_gx, n_gy, planes,
    rows_hbm, now_hbm, start_hbm, hist_hbm, next_hbm, gram_out,
    now, start, result, hist, acc, xhalo, xrest, ysend, yhalo, yedge,
    packed, rs, rs_extra, ex, gat,
    now_sem, start_sem, hist_sem, out_sem, gram_sem,
    xs, xr, ys, yr, rs_s, rs_r, re_s, re_r, ex_s, ex_r, ag_s, ag_r, ae_s, ae_r,
):
    a, c = lax.axis_index("gx"), lax.axis_index("gy")
    n_z = n_gx // LINE
    zz, yy = a // LINE, lax.rem(a, LINE)
    n_near = LINE * n_gy
    me = yy * n_gy + c
    samples = planes // ZSUB
    pairs = hist_hbm.shape[1] // samples
    older = hist_hbm.shape[0]
    load_now = pltpu.make_async_copy(now_hbm, now, now_sem)
    load_start = pltpu.make_async_copy(start_hbm, start, start_sem)
    load_now.start()
    barrier = pltpu.get_barrier_semaphore()
    up, down = lax.rem(a + 1, n_gx), lax.rem(a + n_gx - 1, n_gx)
    ahead, behind = lax.rem(c + 1, n_gy), lax.rem(c + n_gy - 1, n_gy)

    def near_of(d):
        order = lax.rem(d, LINE)
        turn = d // LINE
        dy = jnp.where(order == 0, 2, jnp.where(order == 3, 0, 2 * order - 1))
        other = n_gy - 1 - turn
        dc = jnp.where(other < 2, other, jnp.where(other < 4, other + 4, other - 2))
        y = lax.rem(yy + dy, LINE)
        return y, lax.rem(c + dc, n_gy)

    def far_of(d):
        half = n_z // 2
        dz = jnp.where(lax.rem(d, 2) == 0, half + d // 2, half - 1 - d // 2)
        return lax.rem(zz + dz, n_z)

    def greet(where):
        pl.semaphore_signal(barrier, inc=1, device_id=where, device_id_type=MESH)

    def greet_near(d, carry):
        y, core = near_of(d)
        greet((zz * LINE + y, core))
        return carry

    def greet_far(d, carry):
        greet((far_of(d) * LINE + yy, c))
        return carry

    for where in ((up, c), (down, c), (a, ahead), (a, behind)):
        greet(where)
    lax.fori_loop(0, n_near - 1, greet_near, 0)
    lax.fori_loop(0, n_z - 1, greet_far, 0)

    def load_history(z, carry):
        for i in range(pairs):
            pltpu.make_async_copy(
                hist_hbm.at[:, z * pairs + i], hist.at[z * pairs + i, pl.ds(0, older)], hist_sem.at[z]
            ).start()
        return carry

    lax.fori_loop(0, samples // 2, load_history, 0)
    load_start.start()
    pl.semaphore_wait(barrier, n_near - 1 + n_z - 1 + 4)

    def to(src, dst, send, recv, where):
        return pltpu.make_async_remote_copy(
            src_ref=src, dst_ref=dst, send_sem=send, recv_sem=recv, device_id=where, device_id_type=MESH
        )

    halos = [
        to(rows_hbm.at[:, :, 0, 7], xhalo.at[0], xs.at[0], xr.at[0], (up, c)),
        to(rows_hbm.at[:, :, 0, 0], xhalo.at[1], xs.at[1], xr.at[1], (down, c)),
        to(ysend.at[0], yhalo.at[0, 0], ys.at[0], yr.at[0], (a, ahead)),
        to(ysend.at[0], yhalo.at[0, 1], ys.at[1], yr.at[1], (a, behind)),
    ]
    rest = [
        to(rows_hbm.at[:, :, pl.ds(1, ZSUB - 1), 7], xrest.at[0], xs.at[2], xr.at[2], (up, c)),
        to(rows_hbm.at[:, :, pl.ds(1, ZSUB - 1), 0], xrest.at[1], xs.at[3], xr.at[3], (down, c)),
        to(ysend.at[1], yhalo.at[1, 0], ys.at[2], yr.at[2], (a, ahead)),
        to(ysend.at[1], yhalo.at[1, 1], ys.at[3], yr.at[3], (a, behind)),
    ]
    halos[0].start()
    halos[1].start()
    lane = lax.broadcasted_iota(jnp.int32, (8, 128), 1)
    sub = lax.broadcasted_iota(jnp.int32, (8, 128), 0)
    zero = jnp.zeros((8, 128), jnp.float32)
    load_now.wait()

    def pack_edges(count, stride, where):
        def one(i, carry):
            mask = lax.rem(lane - 2 * i + 129, 128) < 2
            return tuple(
                jnp.where(mask, pltpu.roll(now[f, i * stride], 2 * i, 1), carry[f]) for f in range(5)
            )

        edges = lax.fori_loop(0, count, one, (zero,) * 5, unroll=4)
        for f in range(5):
            ysend[where, f] = edges[f]

    pack_edges(samples, ZSUB, 0)
    halos[2].start()
    halos[3].start()
    rest[0].start()
    rest[1].start()
    lax.fori_loop(samples // 2, samples, load_history, 0)
    pack_edges(planes, 1, 1)
    rest[2].start()
    rest[3].start()

    acc[...] = jnp.zeros_like(acc)

    def block_of(s, count):
        return jnp.concatenate(
            [hist[s * pairs + i].reshape(2 * older + 2, 128) for i in range(pairs * count)], axis=1
        )

    def multiply(s, count):
        block = block_of(s, count)
        for i, j in ((0, 0), (0, 1), (1, 1)):
            rows, cols = slice(256 * i, 256 * i + 256), slice(256 * j, 256 * j + 256)
            product = lax.dot_general(
                block[rows], block[cols], (((1,), (1,)), ((), ())), preferred_element_type=jnp.float32
            )
            acc[2 * j, rows] += product[:, :128]
            acc[2 * j + 1, rows] += product[:, 128:]

    def wait_history(s):
        wait_bytes(hist.at[pl.ds(s * pairs, pairs), pl.ds(0, older)], hist_sem.at[s])

    load_start.wait()
    for copy in halos:
        copy.wait_recv()
    even = lax.rem(lane, 2) == 0

    def merge_edges(which):
        for f in range(5):
            yedge[which, f] = jnp.where(even, yhalo[which, 1, f], yhalo[which, 0, f])

    merge_edges(0)
    xsign = jnp.where(sub == 7, 1.0, -1.0)
    ysign = jnp.where(lane == 127, 1.0, -1.0)

    def load(z):
        return plane_of([now[f, z] for f in range(5)])

    def advance(z, plane, below, above, low, high, which, i):
        p1, n1 = both_of(plane, 1)
        p2, n2 = both_of(plane, 2)
        xe = edge_of([jnp.where(sub < 4, high[f], low[f]) for f in range(5)], 1, xsign)
        turn = lax.rem(128 - 2 * i, 128)
        yq = [pltpu.roll(yedge[which, f], turn, 1) for f in range(5)]
        yq[0] = jnp.where((lane == 0) | (lane == 127), yq[0], 1.0)
        ye = edge_of(yq, 2, ysign)
        fresh = []
        for f in range(5):
            total = below[f] + above[f]
            total += pltpu.roll(jnp.where(sub == 7, xe[f], p1[f]), 1, 0)
            total += pltpu.roll(jnp.where(sub == 0, xe[f], n1[f]), 7, 0)
            total += pltpu.roll(jnp.where(lane == 127, ye[f], p2[f]), 1, 1)
            total += pltpu.roll(jnp.where(lane == 0, ye[f], n2[f]), 127, 1)
            total += 0.75 * start[f, z] + OWN * plane[0][f]
            result[f, z] = total
            fresh.append(total)
        return fresh

    def sampled(s):
        z = s * ZSUB
        below = both_of(load(jnp.maximum(z - 1, 0)), 3)[0]
        above = both_of(load(z + 1), 3)[1]
        low, high = ([xhalo[side, f, s] for f in range(5)] for side in (0, 1))
        fresh = advance(z, load(z), below, above, low, high, 0, s)
        snapshot = pressure_of(fresh, 1.0 / fresh[0]).astype(jnp.bfloat16)
        hist[pl.ds(s * pairs, pairs), older] = snapshot.reshape(pairs, 2, 128)

    def sample_two(i, carry):
        sampled(2 * i)
        sampled(2 * i + 1)
        return carry

    lax.fori_loop(0, GROUP // 2, sample_two, 0)
    for s in range(0, samples, GROUP):
        for t in range(s, s + GROUP):
            wait_history(t)
        multiply(s, GROUP)
        for t in range(s + GROUP, min(s + 2 * GROUP, samples)):
            sampled(t)

    row = lax.broadcasted_iota(jnp.int32, (128, 128), 0)
    col = lax.broadcasted_iota(jnp.int32, (128, 128), 1)

    g00 = fold(acc, 0, 0)
    g01 = fold(acc, 0, 1)
    g11 = fold(acc, 1, 1)
    mixed = jnp.where(col >= row, g11, g00)
    diagonal = jnp.sum(jnp.where(col == row, g00, 0.0), axis=0, keepdims=True)
    for t in range(16):
        packed[t] = mixed[8 * t : 8 * t + 8]
        packed[16 + t] = g01[8 * t : 8 * t + 8]
    packed[n_near] = jnp.broadcast_to(diagonal, (8, 128))

    def scatter(d, carry):
        y, core = near_of(d)
        to(packed.at[y * n_gy + core], rs.at[me], rs_s, rs_r, (zz * LINE + y, core)).start()
        return carry

    @pl.when(me != 0)
    def _():
        to(packed.at[n_near], rs_extra.at[me], re_s, re_r, (zz * LINE, 0)).start()

    lax.fori_loop(0, n_near - 1, scatter, 0, unroll=True)
    rs[me] = packed[me]
    for copy in rest:
        copy.wait_recv()
    merge_edges(1)

    def others(s, carry):
        z0 = s * ZSUB
        parts = [load(z0)]
        below = both_of(parts[0], 3)[0]
        here = load(z0 + 1)
        for k in range(1, ZSUB):
            z = z0 + k
            above = load(jnp.minimum(z + 1, planes - 1))
            low, high = ([xrest[side, f, s, k - 1] for f in range(5)] for side in (0, 1))
            advance(z, here, below, both_of(above, 3)[1], low, high, 1, z)
            below, here = both_of(here, 3)[0], above
        return carry

    def finish(first, last):
        lax.fori_loop(first, last, others, 0)
        part = pl.ds(first * ZSUB, (last - first) * ZSUB)
        pltpu.make_async_copy(result.at[:, part], next_hbm.at[:, part], out_sem).start()

    finish(0, CUTS[0])
    near_rest, far_rest = pl.ds(0, n_near - 1), pl.ds(0, n_z - 1)
    wait_bytes(rs.at[near_rest], rs_r)

    def total_of(ref, count):
        parts = [ref[i] for i in range(count)]
        while len(parts) > 1:
            parts = [sum(parts[i : i + 2]) for i in range(0, len(parts), 2)]
        return parts[0]

    ex[zz, 0] = total_of(rs, n_near)
    ex[zz, 1] = zero

    @pl.when(me == 0)
    def _():
        rs_extra[0] = packed[n_near]
        wait_bytes(rs_extra.at[near_rest], re_r)
        ex[zz, 1] = total_of(rs_extra, n_near)

    def exchange(d, carry):
        to(ex.at[zz], ex.at[zz], ex_s, ex_r, (far_of(d) * LINE + yy, c)).start()
        return carry

    lax.fori_loop(0, n_z - 1, exchange, 0, unroll=True)
    finish(CUTS[0], CUTS[1])
    wait_bytes(ex.at[far_rest], ex_r)
    whole = total_of(ex, n_z)
    gat[me] = whole[0]

    def spread(d, carry):
        y, core = near_of(d)
        to(gat.at[me], gat.at[me], ag_s, ag_r, (zz * LINE + y, core)).start()
        return carry

    @pl.when(me == 0)
    def _():
        gat[n_near] = whole[1]

        def spread_extra(d, carry):
            y, core = near_of(d)
            to(gat.at[n_near], gat.at[n_near], ae_s, ae_r, (zz * LINE + y, core)).start()
            return carry

        lax.fori_loop(0, n_near - 1, spread_extra, 0)

    lax.fori_loop(0, n_near - 1, spread, 0, unroll=True)
    finish(CUTS[1], samples)
    wait_bytes(gat.at[near_rest], ag_r)

    @pl.when(me != 0)
    def _():
        wait_bytes(gat.at[n_near], ae_r)

    hand_on = pltpu.make_async_copy(gat, gram_out, gram_sem)
    hand_on.start()

    @pl.when(me != 0)
    def _():
        wait_bytes(packed.at[n_near], re_s)

    @pl.when(me == 0)
    def _():
        wait_bytes(gat.at[near_rest], ae_s)

    wait_bytes(rs.at[near_rest], rs_s)
    wait_bytes(ex.at[far_rest], ex_s)
    wait_bytes(gat.at[near_rest], ag_s)
    for copy in halos + rest:
        copy.wait_send()
    wait_bytes(result, out_sem)
    hand_on.wait()


def factor(u, out):
    sub = lax.broadcasted_iota(jnp.int32, (8, 128), 0)
    lane = lax.broadcasted_iota(jnp.int32, (8, 128), 1)
    zero = jnp.zeros((8, 128), jnp.float32)
    for b in range(32):
        r0 = 8 * b
        half, off = r0 // 128, r0 % 128
        halves = [0, 1] if half == 0 else [1]
        panel = {h: u[r0 : r0 + 8, 128 * h : 128 * h + 128] for h in halves}
        cols = [jnp.broadcast_to(panel[half][:, off + j : off + j + 1], (8, 128)) for j in range(8)]
        d = {
            (i, j): jnp.broadcast_to(cols[j][i : i + 1, :], (8, 128))
            for j in range(8)
            for i in range(j + 1)
        }
        rows = {h: [jnp.broadcast_to(panel[h][i : i + 1, :], (8, 128)) for i in range(8)] for h in halves}
        chalf = (r0 + 8) // 128
        nh = [h for h in halves if h >= chalf]
        starts = [r0 + 8 * step for step in range(1, AHEAD + 1) if r0 + 8 * step < 256]
        following = [{h: u[n0 : n0 + 8, 128 * h : 128 * h + 128] for h in nh} for n0 in starts]
        g = [
            [
                jnp.broadcast_to(u[n0 : n0 + 8, 128 * half : 128 * half + 128][:, off + j : off + j + 1], (8, 128))
                for j in range(8)
            ]
            for n0 in starts
        ]
        for j in range(8):
            scale = lax.rsqrt(d[j, j])
            for k in range(j + 1, 8):
                d[j, k] = d[j, k] * scale
            for h in halves:
                rows[h][j] = rows[h][j] * scale
            for ahead, values in zip(g, following):
                ahead[j] = ahead[j] * scale
                for h in nh:
                    values[h] = values[h] - ahead[j] * rows[h][j]
            for k in range(j + 1, 8):
                for l in range(k, 8):
                    d[k, l] = d[k, l] - d[j, k] * d[j, l]
                for h in halves:
                    rows[h][k] = rows[h][k] - d[j, k] * rows[h][j]
                for ahead in g:
                    ahead[k] = ahead[k] - d[j, k] * ahead[j]
        done = {}
        for h in halves:
            x = rows[h][7]
            for i in range(7):
                x = jnp.where(sub == i, rows[h][i], x)
            done[h] = x
        for h in (0, 1):
            if h < half:
                value = zero
            elif h == half:
                value = jnp.where(lane >= off + sub, done[h], 0.0)
            else:
                value = done[h]
            out[r0 : r0 + 8, 128 * h : 128 * h + 128] = value
        for n0, values in zip(starts, following):
            for h in nh:
                u[n0 : n0 + 8, 128 * h : 128 * h + 128] = values[h]
        t0 = r0 + 8 + 8 * AHEAD
        if t0 < 256:
            parts = {h: split_of(done[h]) for h in nh}
            c0 = 128 * chalf

            def stack(order):
                return jnp.concatenate(
                    [jnp.concatenate([parts[h][o] for h in nh], axis=1) for o in order], axis=0
                )

            left, right = stack([0, 0, 1, 1, 0, 2]), stack([0, 1, 0, 1, 2, 0])
            product = lax.dot_general(
                left[:, t0 - c0 :], right, (((0,), (0,)), ((), ())), preferred_element_type=jnp.float32
            )
            u[t0:256, c0:256] = u[t0:256, c0:256] - product


def factor_kernel(scale, gram, temp_hbm, next_hbm, triangle, u, held, in_sem, out_sem):
    take = pltpu.make_async_copy(temp_hbm, held, in_sem)
    give = pltpu.make_async_copy(held, next_hbm, out_sem)
    take.start()
    row = lax.broadcasted_iota(jnp.int32, (128, 128), 0)
    col = lax.broadcasted_iota(jnp.int32, (128, 128), 1)
    mixed = gram[0:16].reshape(128, 128) * scale
    cross = gram[16:32].reshape(128, 128) * scale
    diagonal = jnp.broadcast_to(gram[32, 0:1] * scale, (128, 128))
    turned = mixed.T
    u[0:128, 0:128] = jnp.where(col == row, diagonal, jnp.where(col < row, mixed, turned))
    u[128:256, 128:256] = jnp.where(col >= row, mixed, turned)
    u[0:128, 128:256] = cross
    u[128:256, 0:128] = cross.T
    take.wait()
    give.start()
    factor(u, triangle)
    give.wait()


def local(n_gx, n_gy, section_start, section_now, history):
    fields, planes, cx, cy = section_now.shape
    older, samples = history.shape[:2]
    f32, bf16 = jnp.float32, jnp.bfloat16
    any_space = pl.BlockSpec(memory_space=pl.ANY)
    vmem = pl.BlockSpec(memory_space=pltpu.VMEM)
    section = jax.ShapeDtypeStruct(section_now.shape, f32)
    dma = pltpu.SemaphoreType.DMA
    tiles = n_gx + 1
    temp, gram = pl.pallas_call(
        functools.partial(section_kernel, n_gx, n_gy, planes),
        out_shape=(section, jax.ShapeDtypeStruct((tiles, 8, 128), f32)),
        in_specs=[any_space] * 4,
        out_specs=(any_space, any_space),
        scratch_shapes=[
            pltpu.VMEM(section_now.shape, f32),
            pltpu.VMEM(section_now.shape, f32),
            pltpu.VMEM(section_now.shape, f32),
            pltpu.VMEM((samples * cx // 2, older + 1, 2, cy), bf16),
            pltpu.VMEM((4, 2 * older + 2, 128), f32),
            pltpu.VMEM((2, fields, samples, 1, cy), f32),
            pltpu.VMEM((2, fields, samples, ZSUB - 1, 1, cy), f32),
            pltpu.VMEM((2, fields, cx, cy), f32),
            pltpu.VMEM((2, 2, fields, cx, cy), f32),
            pltpu.VMEM((2, fields, cx, cy), f32),
            pltpu.VMEM((tiles, 8, 128), f32),
            pltpu.VMEM((n_gx, 8, 128), f32),
            pltpu.VMEM((n_gx, 8, 128), f32),
            pltpu.VMEM((n_gx // LINE, 2, 8, 128), f32),
            pltpu.VMEM((tiles, 8, 128), f32),
            dma, dma, dma((samples,)), dma, dma,
            dma((4,)), dma((4,)), dma((4,)), dma((4,)),
        ] + [dma] * 10,
        compiler_params=pltpu.CompilerParams(
            collective_id=0, has_side_effects=True, vmem_limit_bytes=60 << 20
        ),
    )(
        section_now.reshape(fields, samples, ZSUB, cx, 1, cy),
        section_now,
        section_start,
        history.reshape(older, samples * cx // 2, 2, cy),
    )
    rows = samples * cx * cy * n_gx * n_gy
    return pl.pallas_call(
        functools.partial(factor_kernel, 1.0 / rows),
        out_shape=(section, jax.ShapeDtypeStruct((older + 1, older + 1), f32)),
        in_specs=[vmem, any_space],
        out_specs=(any_space, vmem),
        scratch_shapes=[
            pltpu.VMEM((older + 1, older + 1), f32),
            pltpu.VMEM(section_now.shape, f32),
            dma, dma,
        ],
    )(gram, temp)


def solution(mesh):
    spec = P(None, None, "gx", "gy")
    return jax.shard_map(
        functools.partial(local, mesh.shape["gx"], mesh.shape["gy"]),
        mesh=mesh,
        in_specs=(spec, spec, spec),
        out_specs=(spec, P()),
        check_vma=False,
    )
```

```python
import functools

import jax
import jax.numpy as jnp
from jax import lax
from jax.experimental import pallas as pl
from jax.experimental.pallas import tpu as pltpu
from jax.sharding import PartitionSpec as P

ZSUB = 4
LINE = 4
GROUP = 4
AHEAD = 3
CUTS = (6, 10)
GAMMA_LESS = 0.4
TIME_STEP = 0.2
VISCOUS = 0.25
MESH = pl.DeviceIdType.MESH
FLUX = 0.25 * TIME_STEP * 0.5
NEAR = 0.25 * TIME_STEP * VISCOUS
OWN = 0.25 - 6.0 * NEAR


def wait_bytes(ref, sem):
    pltpu.make_async_copy(ref, ref, sem).wait()


def pressure_of(q, inverse):
    kinetic = q[1] * q[1] + q[2] * q[2] + q[3] * q[3]
    return GAMMA_LESS * (q[4] - 0.5 * kinetic * inverse)


def plane_of(q):
    inverse = 1.0 / q[0]
    pressure = pressure_of(q, inverse)
    return q, inverse * FLUX, pressure * FLUX, q[4] + pressure


def flux_of(plane, k, sign=None):
    q, scaled, pressure, enthalpy = plane
    if sign is not None:
        scaled, pressure = scaled * sign, pressure * sign
    velocity = q[k] * scaled
    flux = [q[0] * velocity]
    for member in (1, 2, 3):
        term = q[member] * velocity
        flux.append(term + pressure if member == k else term)
    flux.append(enthalpy * velocity)
    return flux


def both_of(plane, k):
    flux = flux_of(plane, k)
    base = [NEAR * value for value in plane[0]]
    return [b + f for b, f in zip(base, flux)], [b - f for b, f in zip(base, flux)]


def edge_of(q, k, sign):
    flux = flux_of(plane_of(q), k, sign)
    return [NEAR * value + f for value, f in zip(q, flux)]


def fold(acc, first, second):
    row = lax.broadcasted_iota(jnp.int32, (256, 128), 0)
    col = lax.broadcasted_iota(jnp.int32, (256, 128), 1)
    total = jnp.zeros((128, 128), jnp.float32)
    for parity in (0, 1):
        pick = (row == 2 * col + parity).astype(jnp.bfloat16)
        for h in (0, 1):
            part = acc[2 * second + h, pl.ds(256 * first + parity, 128, stride=2), :]
            chosen = pick[128 * h : 128 * h + 128]
            for piece in split_of(part):
                total = total + jnp.dot(piece, chosen, preferred_element_type=jnp.float32)
    return total


def split_of(x):
    high = x.astype(jnp.bfloat16)
    rest = x - high.astype(jnp.float32)
    middle = rest.astype(jnp.bfloat16)
    low = (rest - middle.astype(jnp.float32)).astype(jnp.bfloat16)
    return high, middle, low


def section_kernel(
    n_gx, n_gy, planes,
    rows_hbm, now_hbm, start_hbm, hist_hbm, next_hbm, gram_out,
    now, start, result, hist, acc, xhalo, xrest, ysend, yhalo, yedge,
    packed, rs, rs_extra, ex, gat,
    now_sem, start_sem, hist_sem, out_sem, gram_sem,
    xs, xr, ys, yr, rs_s, rs_r, re_s, re_r, ex_s, ex_r, ag_s, ag_r, ae_s, ae_r,
):
    a, c = lax.axis_index("gx"), lax.axis_index("gy")
    n_z = n_gx // LINE
    zz, yy = a // LINE, lax.rem(a, LINE)
    n_near = LINE * n_gy
    me = yy * n_gy + c
    samples = planes // ZSUB
    pairs = hist_hbm.shape[1] // samples
    older = hist_hbm.shape[0]
    load_now = pltpu.make_async_copy(now_hbm, now, now_sem)
    load_start = pltpu.make_async_copy(start_hbm, start, start_sem)
    load_now.start()
    barrier = pltpu.get_barrier_semaphore()
    up, down = lax.rem(a + 1, n_gx), lax.rem(a + n_gx - 1, n_gx)
    ahead, behind = lax.rem(c + 1, n_gy), lax.rem(c + n_gy - 1, n_gy)

    def near_of(d):
        order = lax.rem(d, LINE)
        turn = d // LINE
        dy = jnp.where(order == 0, 2, jnp.where(order == 3, 0, 2 * order - 1))
        other = n_gy - 1 - turn
        dc = jnp.where(other < 2, other, jnp.where(other < 4, other + 4, other - 2))
        y = lax.rem(yy + dy, LINE)
        return y, lax.rem(c + dc, n_gy)

    def far_of(d):
        half = n_z // 2
        dz = jnp.where(lax.rem(d, 2) == 0, half + d // 2, half - 1 - d // 2)
        return lax.rem(zz + dz, n_z)

    def greet(where):
        pl.semaphore_signal(barrier, inc=1, device_id=where, device_id_type=MESH)

    def greet_near(d, carry):
        y, core = near_of(d)
        greet((zz * LINE + y, core))
        return carry

    def greet_far(d, carry):
        greet((far_of(d) * LINE + yy, c))
        return carry

    for where in ((up, c), (down, c), (a, ahead), (a, behind)):
        greet(where)
    lax.fori_loop(0, n_near - 1, greet_near, 0)
    lax.fori_loop(0, n_z - 1, greet_far, 0)

    def load_history(z, carry):
        for i in range(pairs):
            pltpu.make_async_copy(
                hist_hbm.at[:, z * pairs + i], hist.at[z * pairs + i, pl.ds(0, older)], hist_sem.at[z]
            ).start()
        return carry

    lax.fori_loop(0, samples, load_history, 0)
    load_start.start()

    def to(src, dst, send, recv, where):
        return pltpu.make_async_remote_copy(
            src_ref=src, dst_ref=dst, send_sem=send, recv_sem=recv, device_id=where, device_id_type=MESH
        )

    halos = [
        to(rows_hbm.at[:, :, 0, 7], xhalo.at[0], xs.at[0], xr.at[0], (up, c)),
        to(rows_hbm.at[:, :, 0, 0], xhalo.at[1], xs.at[1], xr.at[1], (down, c)),
        to(ysend.at[0], yhalo.at[0, 0], ys.at[0], yr.at[0], (a, ahead)),
        to(ysend.at[0], yhalo.at[0, 1], ys.at[1], yr.at[1], (a, behind)),
    ]
    rest = [
        to(rows_hbm.at[:, :, pl.ds(1, ZSUB - 1), 7], xrest.at[0], xs.at[2], xr.at[2], (up, c)),
        to(rows_hbm.at[:, :, pl.ds(1, ZSUB - 1), 0], xrest.at[1], xs.at[3], xr.at[3], (down, c)),
        to(ysend.at[1], yhalo.at[1, 0], ys.at[2], yr.at[2], (a, ahead)),
        to(ysend.at[1], yhalo.at[1, 1], ys.at[3], yr.at[3], (a, behind)),
    ]
    lane = lax.broadcasted_iota(jnp.int32, (8, 128), 1)
    sub = lax.broadcasted_iota(jnp.int32, (8, 128), 0)
    zero = jnp.zeros((8, 128), jnp.float32)
    load_now.wait()

    def pack_edges(count, stride, where):
        def one(i, carry):
            mask = lax.rem(lane - 2 * i + 129, 128) < 2
            return tuple(
                jnp.where(mask, pltpu.roll(now[f, i * stride], 2 * i, 1), carry[f]) for f in range(5)
            )

        edges = lax.fori_loop(0, count, one, (zero,) * 5, unroll=4)
        for f in range(5):
            ysend[where, f] = edges[f]

    pack_edges(samples, ZSUB, 0)
    pack_edges(planes, 1, 1)
    acc[...] = jnp.zeros_like(acc)
    pl.semaphore_wait(barrier, n_near - 1 + n_z - 1 + 4)
    for copy in halos:
        copy.start()

    def block_of(s, count):
        return jnp.concatenate(
            [hist[s * pairs + i].reshape(2 * older + 2, 128) for i in range(pairs * count)], axis=1
        )

    def multiply(s, count):
        block = block_of(s, count)
        for i, j in ((0, 0), (0, 1), (1, 1)):
            rows, cols = slice(256 * i, 256 * i + 256), slice(256 * j, 256 * j + 256)
            product = lax.dot_general(
                block[rows], block[cols], (((1,), (1,)), ((), ())), preferred_element_type=jnp.float32
            )
            acc[2 * j, rows] += product[:, :128]
            acc[2 * j + 1, rows] += product[:, 128:]

    def wait_history(s):
        wait_bytes(hist.at[pl.ds(s * pairs, pairs), pl.ds(0, older)], hist_sem.at[s])

    load_start.wait()
    for copy in halos:
        copy.wait_recv()
    for copy in rest:
        copy.start()
    even = lax.rem(lane, 2) == 0

    def merge_edges(which):
        for f in range(5):
            yedge[which, f] = jnp.where(even, yhalo[which, 1, f], yhalo[which, 0, f])

    merge_edges(0)
    xsign = jnp.where(sub == 7, 1.0, -1.0)
    ysign = jnp.where(lane == 127, 1.0, -1.0)

    def load(z):
        return plane_of([now[f, z] for f in range(5)])

    def advance(z, plane, below, above, low, high, which, i):
        p1, n1 = both_of(plane, 1)
        p2, n2 = both_of(plane, 2)
        xe = edge_of([jnp.where(sub < 4, high[f], low[f]) for f in range(5)], 1, xsign)
        turn = lax.rem(128 - 2 * i, 128)
        yq = [pltpu.roll(yedge[which, f], turn, 1) for f in range(5)]
        yq[0] = jnp.where((lane == 0) | (lane == 127), yq[0], 1.0)
        ye = edge_of(yq, 2, ysign)
        fresh = []
        for f in range(5):
            total = below[f] + above[f]
            total += pltpu.roll(jnp.where(sub == 7, xe[f], p1[f]), 1, 0)
            total += pltpu.roll(jnp.where(sub == 0, xe[f], n1[f]), 7, 0)
            total += pltpu.roll(jnp.where(lane == 127, ye[f], p2[f]), 1, 1)
            total += pltpu.roll(jnp.where(lane == 0, ye[f], n2[f]), 127, 1)
            total += 0.75 * start[f, z] + OWN * plane[0][f]
            result[f, z] = total
            fresh.append(total)
        return fresh

    def sampled(s):
        z = s * ZSUB
        below = both_of(load(jnp.maximum(z - 1, 0)), 3)[0]
        above = both_of(load(z + 1), 3)[1]
        low, high = ([xhalo[side, f, s] for f in range(5)] for side in (0, 1))
        fresh = advance(z, load(z), below, above, low, high, 0, s)
        snapshot = pressure_of(fresh, 1.0 / fresh[0]).astype(jnp.bfloat16)
        hist[pl.ds(s * pairs, pairs), older] = snapshot.reshape(pairs, 2, 128)

    def sample_two(i, carry):
        sampled(2 * i)
        sampled(2 * i + 1)
        return carry

    lax.fori_loop(0, GROUP // 2, sample_two, 0)
    for s in range(0, samples, GROUP):
        for t in range(s, s + GROUP):
            wait_history(t)
        multiply(s, GROUP)
        for t in range(s + GROUP, min(s + 2 * GROUP, samples)):
            sampled(t)

    row = lax.broadcasted_iota(jnp.int32, (128, 128), 0)
    col = lax.broadcasted_iota(jnp.int32, (128, 128), 1)

    g00 = fold(acc, 0, 0)
    g01 = fold(acc, 0, 1)
    g11 = fold(acc, 1, 1)
    mixed = jnp.where(col >= row, g11, g00)
    diagonal = jnp.sum(jnp.where(col == row, g00, 0.0), axis=0, keepdims=True)
    for t in range(16):
        packed[t] = mixed[8 * t : 8 * t + 8]
        packed[16 + t] = g01[8 * t : 8 * t + 8]
    packed[n_near] = jnp.broadcast_to(diagonal, (8, 128))

    def scatter(d, carry):
        y, core = near_of(d)
        to(packed.at[y * n_gy + core], rs.at[me], rs_s, rs_r, (zz * LINE + y, core)).start()
        return carry

    @pl.when(me != 0)
    def _():
        to(packed.at[n_near], rs_extra.at[me], re_s, re_r, (zz * LINE, 0)).start()

    lax.fori_loop(0, n_near - 1, scatter, 0, unroll=True)
    rs[me] = packed[me]
    for copy in rest:
        copy.wait_recv()
    merge_edges(1)

    def others(s, carry):
        z0 = s * ZSUB
        parts = [load(z0)]
        below = both_of(parts[0], 3)[0]
        here = load(z0 + 1)
        for k in range(1, ZSUB):
            z = z0 + k
            above = load(jnp.minimum(z + 1, planes - 1))
            low, high = ([xrest[side, f, s, k - 1] for f in range(5)] for side in (0, 1))
            advance(z, here, below, both_of(above, 3)[1], low, high, 1, z)
            below, here = both_of(here, 3)[0], above
        return carry

    def finish(first, last):
        lax.fori_loop(first, last, others, 0)
        part = pl.ds(first * ZSUB, (last - first) * ZSUB)
        pltpu.make_async_copy(result.at[:, part], next_hbm.at[:, part], out_sem).start()

    finish(0, CUTS[0])
    near_rest, far_rest = pl.ds(0, n_near - 1), pl.ds(0, n_z - 1)
    wait_bytes(rs.at[near_rest], rs_r)

    def total_of(ref, count):
        parts = [ref[i] for i in range(count)]
        while len(parts) > 1:
            parts = [sum(parts[i : i + 2]) for i in range(0, len(parts), 2)]
        return parts[0]

    ex[zz, 0] = total_of(rs, n_near)
    ex[zz, 1] = zero

    @pl.when(me == 0)
    def _():
        rs_extra[0] = packed[n_near]
        wait_bytes(rs_extra.at[near_rest], re_r)
        ex[zz, 1] = total_of(rs_extra, n_near)

    def exchange(d, carry):
        to(ex.at[zz], ex.at[zz], ex_s, ex_r, (far_of(d) * LINE + yy, c)).start()
        return carry

    lax.fori_loop(0, n_z - 1, exchange, 0, unroll=True)
    finish(CUTS[0], CUTS[1])
    wait_bytes(ex.at[far_rest], ex_r)
    whole = total_of(ex, n_z)
    gat[me] = whole[0]

    def spread(d, carry):
        y, core = near_of(d)
        to(gat.at[me], gat.at[me], ag_s, ag_r, (zz * LINE + y, core)).start()
        return carry

    @pl.when(me == 0)
    def _():
        gat[n_near] = whole[1]

        def spread_extra(d, carry):
            y, core = near_of(d)
            to(gat.at[n_near], gat.at[n_near], ae_s, ae_r, (zz * LINE + y, core)).start()
            return carry

        lax.fori_loop(0, n_near - 1, spread_extra, 0)

    lax.fori_loop(0, n_near - 1, spread, 0, unroll=True)
    finish(CUTS[1], samples)
    wait_bytes(gat.at[near_rest], ag_r)

    @pl.when(me != 0)
    def _():
        wait_bytes(gat.at[n_near], ae_r)

    hand_on = pltpu.make_async_copy(gat, gram_out, gram_sem)
    hand_on.start()

    @pl.when(me != 0)
    def _():
        wait_bytes(packed.at[n_near], re_s)

    @pl.when(me == 0)
    def _():
        wait_bytes(gat.at[near_rest], ae_s)

    wait_bytes(rs.at[near_rest], rs_s)
    wait_bytes(ex.at[far_rest], ex_s)
    wait_bytes(gat.at[near_rest], ag_s)
    for copy in halos + rest:
        copy.wait_send()
    wait_bytes(result, out_sem)
    hand_on.wait()


def factor(u, out):
    sub = lax.broadcasted_iota(jnp.int32, (8, 128), 0)
    lane = lax.broadcasted_iota(jnp.int32, (8, 128), 1)
    zero = jnp.zeros((8, 128), jnp.float32)
    for b in range(32):
        r0 = 8 * b
        half, off = r0 // 128, r0 % 128
        halves = [0, 1] if half == 0 else [1]
        panel = {h: u[r0 : r0 + 8, 128 * h : 128 * h + 128] for h in halves}
        cols = [jnp.broadcast_to(panel[half][:, off + j : off + j + 1], (8, 128)) for j in range(8)]
        d = {
            (i, j): jnp.broadcast_to(cols[j][i : i + 1, :], (8, 128))
            for j in range(8)
            for i in range(j + 1)
        }
        rows = {h: [jnp.broadcast_to(panel[h][i : i + 1, :], (8, 128)) for i in range(8)] for h in halves}
        chalf = (r0 + 8) // 128
        nh = [h for h in halves if h >= chalf]
        starts = [r0 + 8 * step for step in range(1, AHEAD + 1) if r0 + 8 * step < 256]
        following = [{h: u[n0 : n0 + 8, 128 * h : 128 * h + 128] for h in nh} for n0 in starts]
        g = [
            [
                jnp.broadcast_to(u[n0 : n0 + 8, 128 * half : 128 * half + 128][:, off + j : off + j + 1], (8, 128))
                for j in range(8)
            ]
            for n0 in starts
        ]
        for j in range(8):
            scale = lax.rsqrt(d[j, j])
            for k in range(j + 1, 8):
                d[j, k] = d[j, k] * scale
            for h in halves:
                rows[h][j] = rows[h][j] * scale
            for ahead, values in zip(g, following):
                ahead[j] = ahead[j] * scale
                for h in nh:
                    values[h] = values[h] - ahead[j] * rows[h][j]
            for k in range(j + 1, 8):
                for l in range(k, 8):
                    d[k, l] = d[k, l] - d[j, k] * d[j, l]
                for h in halves:
                    rows[h][k] = rows[h][k] - d[j, k] * rows[h][j]
                for ahead in g:
                    ahead[k] = ahead[k] - d[j, k] * ahead[j]
        done = {}
        for h in halves:
            x = rows[h][7]
            for i in range(7):
                x = jnp.where(sub == i, rows[h][i], x)
            done[h] = x
        for h in (0, 1):
            if h < half:
                value = zero
            elif h == half:
                value = jnp.where(lane >= off + sub, done[h], 0.0)
            else:
                value = done[h]
            out[r0 : r0 + 8, 128 * h : 128 * h + 128] = value
        for n0, values in zip(starts, following):
            for h in nh:
                u[n0 : n0 + 8, 128 * h : 128 * h + 128] = values[h]
        t0 = r0 + 8 + 8 * AHEAD
        if t0 < 256:
            parts = {h: split_of(done[h]) for h in nh}
            c0 = 128 * chalf

            def stack(order):
                return jnp.concatenate(
                    [jnp.concatenate([parts[h][o] for h in nh], axis=1) for o in order], axis=0
                )

            left, right = stack([0, 0, 1, 1, 0, 2]), stack([0, 1, 0, 1, 2, 0])
            product = lax.dot_general(
                left[:, t0 - c0 :], right, (((0,), (0,)), ((), ())), preferred_element_type=jnp.float32
            )
            u[t0:256, c0:256] = u[t0:256, c0:256] - product


def factor_kernel(scale, gram, temp_hbm, next_hbm, triangle, u, held, in_sem, out_sem):
    take = pltpu.make_async_copy(temp_hbm, held, in_sem)
    give = pltpu.make_async_copy(held, next_hbm, out_sem)
    take.start()
    row = lax.broadcasted_iota(jnp.int32, (128, 128), 0)
    col = lax.broadcasted_iota(jnp.int32, (128, 128), 1)
    mixed = gram[0:16].reshape(128, 128) * scale
    cross = gram[16:32].reshape(128, 128) * scale
    diagonal = jnp.broadcast_to(gram[32, 0:1] * scale, (128, 128))
    turned = mixed.T
    u[0:128, 0:128] = jnp.where(col == row, diagonal, jnp.where(col < row, mixed, turned))
    u[128:256, 128:256] = jnp.where(col >= row, mixed, turned)
    u[0:128, 128:256] = cross
    u[128:256, 0:128] = cross.T
    take.wait()
    give.start()
    factor(u, triangle)
    give.wait()


def local(n_gx, n_gy, section_start, section_now, history):
    fields, planes, cx, cy = section_now.shape
    older, samples = history.shape[:2]
    f32, bf16 = jnp.float32, jnp.bfloat16
    any_space = pl.BlockSpec(memory_space=pl.ANY)
    vmem = pl.BlockSpec(memory_space=pltpu.VMEM)
    section = jax.ShapeDtypeStruct(section_now.shape, f32)
    dma = pltpu.SemaphoreType.DMA
    tiles = n_gx + 1
    temp, gram = pl.pallas_call(
        functools.partial(section_kernel, n_gx, n_gy, planes),
        out_shape=(section, jax.ShapeDtypeStruct((tiles, 8, 128), f32)),
        in_specs=[any_space] * 4,
        out_specs=(any_space, any_space),
        scratch_shapes=[
            pltpu.VMEM(section_now.shape, f32),
            pltpu.VMEM(section_now.shape, f32),
            pltpu.VMEM(section_now.shape, f32),
            pltpu.VMEM((samples * cx // 2, older + 1, 2, cy), bf16),
            pltpu.VMEM((4, 2 * older + 2, 128), f32),
            pltpu.VMEM((2, fields, samples, 1, cy), f32),
            pltpu.VMEM((2, fields, samples, ZSUB - 1, 1, cy), f32),
            pltpu.VMEM((2, fields, cx, cy), f32),
            pltpu.VMEM((2, 2, fields, cx, cy), f32),
            pltpu.VMEM((2, fields, cx, cy), f32),
            pltpu.VMEM((tiles, 8, 128), f32),
            pltpu.VMEM((n_gx, 8, 128), f32),
            pltpu.VMEM((n_gx, 8, 128), f32),
            pltpu.VMEM((n_gx // LINE, 2, 8, 128), f32),
            pltpu.VMEM((tiles, 8, 128), f32),
            dma, dma, dma((samples,)), dma, dma,
            dma((4,)), dma((4,)), dma((4,)), dma((4,)),
        ] + [dma] * 10,
        compiler_params=pltpu.CompilerParams(
            collective_id=0, has_side_effects=True, vmem_limit_bytes=60 << 20
        ),
    )(
        section_now.reshape(fields, samples, ZSUB, cx, 1, cy),
        section_now,
        section_start,
        history.reshape(older, samples * cx // 2, 2, cy),
    )
    rows = samples * cx * cy * n_gx * n_gy
    return pl.pallas_call(
        functools.partial(factor_kernel, 1.0 / rows),
        out_shape=(section, jax.ShapeDtypeStruct((older + 1, older + 1), f32)),
        in_specs=[vmem, any_space],
        out_specs=(any_space, vmem),
        scratch_shapes=[
            pltpu.VMEM((older + 1, older + 1), f32),
            pltpu.VMEM(section_now.shape, f32),
            dma, dma,
        ],
    )(gram, temp)


def solution(mesh):
    spec = P(None, None, "gx", "gy")
    return jax.shard_map(
        functools.partial(local, mesh.shape["gx"], mesh.shape["gy"]),
        mesh=mesh,
        in_specs=(spec, spec, spec),
        out_specs=(spec, P()),
        check_vma=False,
    )
```
